32 devices in a mesh: groups: 2 (over y), cells: 4 (over z), corners: 2 (over x), kern: 2 (over core).
Axes of the slice: x: 2, y: 2, z: 4, core: 2. Of those that a mesh axis runs over, the one named last changes fastest.
Arguments:
- theta: float32 [64, 128, 128], P(('groups', 'cells')), parts along dimension 0, may hold values from -8 to 8
- target: bfloat16 [16, 128, 128], P(('groups', 'cells')), parts along dimension 0, may hold values from 0 to 1
- kernels: float32 [2, 2, 24, 35, 35], P(None, 'corners', 'kern'), may hold values from -25.33743 to 25.33743
- dose: float32 [2], P('corners'), may hold values from 0.6 to 1
- inst_owner: int32 [128, 1], P(('groups', 'cells')), parts along dimension 0, may hold values from 0 to 3; in each aligned block of 16 rows (0 to 15, 16 to 31, ...) at most 8 rows name the same one
- inst_local: int32 [128], P(('groups', 'cells')), parts along dimension 0, may hold values from 0 to 7
- inst_shift: int32 [128], P(('groups', 'cells')), parts along dimension 0, may hold values from 0 to 127
Outputs:
- theta_out: float32 [64, 128, 128], P(('groups', 'cells'), ('corners', 'kern')), parts along dimension 0
The draws below stay inside these ranges and needn't reach their ends.
There are 2 independent parts, one for each index of `groups`. The reference program is written for one: setup_inputs(seed, part) draws one part's arguments, and reference() takes and returns one part's arrays. A program takes and returns all parts, laid end to end along the dimension named above; an argument that names none is the same for every part. Nothing has to cross between parts.
Inputs may be any that keep to these rules, and one draw needn't show every extreme that they name: `inst_owner`: within the rows of one device (aligned blocks of 16 rows) no owner is named by more than 8 rows, and in some block one owner is named by exactly 8.
All inputs are finite; a program needn't handle non-finite values.
Results may differ from the reference program's by a relative error of at most 0.003.
Values may be sent and summed in bfloat16 or wider, within the bound.
A program may use at most 64 MiB of HBM per device.

```python
import math
import jax
import jax.numpy as jnp
import numpy as np
from jax import lax

CELL = 128
FREQ = 35
CELLS_DEV = 8
SLOTS = 8
ITERS = 2
KERNELS = 24
CORNERS = 2
CELLS = 32
TILES = 8
INST_DEV = 16
INSTANCES = 64
CAP = 8
N_CELLS = 4


def with_ends(array, own_key, low, largest):
    extent = array.shape
    spot = [jax.random.randint(jax.random.fold_in(own_key, axis), (), 0, extent[axis]) for axis in range(len(extent))]
    array = array.at[tuple(spot)].set(low)
    longest = extent.index(max(extent))
    spot[longest] = (spot[longest] + 1) % extent[longest]
    return array.at[tuple(spot)].set(largest)


def level_of(rng, extent, cuts, smallest, high):
    factor_of, own = 1.0, jax.random.fold_in(rng, 6)
    for axis_at, shards_of in cuts:
        draws = jnp.exp(jax.random.uniform(jax.random.fold_in(own, axis_at), (shards_of,), jnp.float32, smallest / len(cuts), high / len(cuts)))
        factor_of = factor_of * jnp.repeat(draws, extent[axis_at] // shards_of).reshape([-1 if axis == axis_at else 1 for axis in range(len(extent))])
    return factor_of


def deal_out(key, own, number, rows, amount, top, reach, lean):
    order = jax.random.permutation(key, amount)
    heavy_load, common = portions_of(amount, rows * top, reach, lean, True), portions_of(amount, rows * top, reach, lean, False)
    places = jnp.arange(amount)

    def named(sizes, offset_by):
        used = int((sizes > 0).sum())
        fixed = max(1, used // 4)
        passed = fixed + (places - fixed + offset_by * (used - fixed)) % max(1, amount - fixed)
        return jnp.zeros((amount,), jnp.int32).at[order[jnp.where(places < fixed, places, passed)]].set(jnp.asarray(sizes, jnp.int32))

    sizes = jnp.where(number % 4 == 0, named(heavy_load, number // 4), named(common, number - number // 4 - 1))
    mixed = jax.random.permutation(jax.random.fold_in(own, 3), amount)
    donor, receiver = mixed[0:amount // 2 * 2:2], mixed[1:amount // 2 * 2:2]
    slack = jnp.minimum(sizes[donor] - 1, reach - sizes[receiver]) // 2
    slack = jnp.where((donor == order[0]) | (receiver == order[0]) | (sizes[receiver] == 0), 0, jnp.maximum(slack, 0))
    passed = jax.random.randint(jax.random.fold_in(own, 4), (amount // 2,), 0, 1 << 20) % (slack + 1)
    sizes = sizes.at[donor].add(-passed).at[receiver].add(passed)
    items = jnp.searchsorted(jnp.cumsum(sizes), jnp.arange(rows * top), side="right").astype(jnp.int32)
    table = items.reshape(top, rows).T
    table = table[jax.random.permutation(jax.random.fold_in(own, 1), rows)]
    offset_by = jax.random.randint(jax.random.fold_in(own, 2), (rows, 1), 0, top)
    return jnp.take_along_axis(table, (jnp.arange(top)[None, :] + offset_by) % top, axis=1)


def portions_of(amount, total, most, slope, full):
    weights = [(1 << 20) // math.isqrt(rank ** slope) + 1 for rank in range(1, amount + 1)]
    largest = most if full else min(most, max(-(-total // amount), total * weights[0] // sum(weights)))
    least = 1 if total - largest >= amount - 1 else 0
    counts, surplus = [largest] + [least] * (amount - 1), total - largest - least * (amount - 1)
    while surplus > 0:
        movable = [i for i in range(1, amount) if counts[i] < largest] or [i for i in range(1, amount) if counts[i] < most]
        whole, budget = sum([weights[i] for i in movable]), surplus
        for i in movable:
            extra = min(most - counts[i], max(1, budget * weights[i] // whole), surplus)
            counts[i] = counts[i] + extra
            surplus = surplus - extra
    return np.array(counts)


def scatter_about(key, dims, spread, limit, cuts=(), held_as=jnp.bfloat16):
    array = jax.random.normal(key, dims, jnp.float32) * spread
    if len(cuts) > 0:
        array = level_of(key, dims, cuts, -0.22, 0.18) * array
    return jnp.clip(array, min=-limit, max=limit).astype(held_as)


def setup_inputs(seed: int = 0, part: int = 0) -> dict:
    seeds = jax.random.split(jax.random.key(seed), 8)
    part_keys = jax.random.split(jax.random.fold_in(seeds[7], part), 8)
    theta = scatter_about(part_keys[0], (CELLS, CELL, CELL), 2.0, 8.0, ((0, 4),), jnp.float32)
    target = jnp.clip(1.0 * jax.random.uniform(part_keys[1], (TILES, CELL, CELL), jnp.float32) ** level_of(part_keys[1], (TILES, CELL, CELL), ((0, 4),), -0.2, 0.2), 0.0, 1.0).astype(jnp.bfloat16)
    kernels = scatter_about(seeds[2], (2, CORNERS, KERNELS, FREQ, FREQ), (2.0 * CELL * SLOTS ** 0.5 / (FREQ * KERNELS ** 0.5)), 25.33743, ((1, 2), (2, 2)), jnp.float32)
    dose = jnp.clip(0.6 + 0.39999998 * jax.random.uniform(seeds[3], (CORNERS,), jnp.float32) ** level_of(seeds[3], (CORNERS,), ((0, 2),), -0.2, 0.2), 0.6, 1.0)
    inst_owner_keys = jax.random.split(jax.random.fold_in(part_keys[4], 1), INSTANCES // INST_DEV)
    inst_owner_turns = jax.random.permutation(jax.random.fold_in(part_keys[4], 3), INSTANCES // INST_DEV)
    inst_owner = jax.vmap(lambda own, number: deal_out(jax.random.fold_in(part_keys[4], 2), own, number, INST_DEV, N_CELLS, 1, CAP, 2))(inst_owner_keys, inst_owner_turns).reshape((INSTANCES, 1))
    inst_local = with_ends(jax.random.randint(part_keys[5], (INSTANCES,), 0, CELLS_DEV), jax.random.fold_in(part_keys[5], 1), 0, CELLS_DEV - 1).astype(jnp.int32)
    inst_shift = with_ends(jax.random.randint(part_keys[6], (INSTANCES,), 0, CELL), jax.random.fold_in(part_keys[6], 1), 0, CELL - 1).astype(jnp.int32)
    return {"theta": theta, "target": target, "kernels": kernels, "dose": dose, "inst_owner": inst_owner, "inst_local": inst_local, "inst_shift": inst_shift}


LR = 0.25
EPS = 1e-06
STEEP = 3.0

def tables(cell_size, freq_count):
    freqs = jnp.arange(freq_count, dtype=jnp.int32) - freq_count // 2
    pixels = jnp.arange(cell_size, dtype=jnp.int32)
    phase = (freqs[:, None] * pixels[None, :] % cell_size).astype(jnp.float32) * (2.0 * math.pi / cell_size)
    fwd_real = jnp.cos(phase)
    fwd_imag = -jnp.sin(phase)
    inv_real = fwd_real.T / cell_size
    inv_imag = -fwd_imag.T / cell_size
    return (fwd_real, fwd_imag, inv_real, inv_imag)

def spectrum(field, tabs):
    fwd_real, fwd_imag = (tabs[0], tabs[1])
    hp = lax.Precision.HIGHEST
    left_real = jnp.einsum('fx,txy->tfy', fwd_real, field, precision=hp)
    left_imag = jnp.einsum('fx,txy->tfy', fwd_imag, field, precision=hp)
    spec_real = jnp.einsum('tfy,gy->tfg', left_real, fwd_real, precision=hp) - jnp.einsum('tfy,gy->tfg', left_imag, fwd_imag, precision=hp)
    spec_imag = jnp.einsum('tfy,gy->tfg', left_real, fwd_imag, precision=hp) + jnp.einsum('tfy,gy->tfg', left_imag, fwd_real, precision=hp)
    return (spec_real, spec_imag)

def intensity(field, kern_real, kern_imag, tabs):
    inv_real, inv_imag = (tabs[2], tabs[3])
    hp = lax.Precision.HIGHEST
    spec_real, spec_imag = spectrum(field, tabs)

    def add_kernel(running, pair):
        resp_real = pair[0] * spec_real - pair[1] * spec_imag
        resp_imag = pair[0] * spec_imag + pair[1] * spec_real
        half_real = jnp.einsum('tfg,yg->tfy', resp_real, inv_real, precision=hp) - jnp.einsum('tfg,yg->tfy', resp_imag, inv_imag, precision=hp)
        half_imag = jnp.einsum('tfg,yg->tfy', resp_real, inv_imag, precision=hp) + jnp.einsum('tfg,yg->tfy', resp_imag, inv_real, precision=hp)
        near_real = jnp.einsum('xf,tfy->txy', inv_real, half_real, precision=hp) - jnp.einsum('xf,tfy->txy', inv_imag, half_imag, precision=hp)
        near_imag = jnp.einsum('xf,tfy->txy', inv_real, half_imag, precision=hp) + jnp.einsum('xf,tfy->txy', inv_imag, half_real, precision=hp)
        return (running + near_real * near_real + near_imag * near_imag, None)
    start = jnp.zeros(field.shape, jnp.float32)
    result, unused = lax.scan(add_kernel, start, (kern_real, kern_imag))
    return result

def reference(theta, target, kernels, dose, inst_owner, inst_local, inst_shift):
    tabs = tables(CELL, FREQ)
    cell_ids = (inst_owner[:, 0] * CELLS_DEV + inst_local).astype(jnp.int32)
    wanted = target.astype(jnp.float32)

    def build(cell_params):
        rounded = jax.nn.sigmoid(cell_params).astype(jnp.bfloat16)
        mask_vals = lax.optimization_barrier(rounded).astype(jnp.float32)
        placed = jnp.take(2.0 * mask_vals - 1.0, cell_ids, axis=0)
        rolled = jax.vmap(lambda plane, offset: jnp.roll(plane, offset, axis=1))(placed, inst_shift)
        return lax.optimization_barrier(jnp.sum(rolled.reshape(TILES, SLOTS, CELL, CELL), axis=1)) / SLOTS
    cell_params = theta
    for iteration in range(ITERS):
        field = build(cell_params)

        def corner_grad(inputs):
            kern_real, kern_imag, dose_now = inputs
            image, pullback = jax.vjp(lambda plane: intensity(plane, kern_real, kern_imag, tabs), field)
            resist = jax.nn.sigmoid(STEEP * (dose_now * image - 1.0))
            pressure = 2.0 * (resist - wanted) * resist * (1.0 - resist) * STEEP * dose_now
            return pullback(pressure)[0]
        tile_grads = lax.optimization_barrier(jnp.sum(lax.map(corner_grad, (kernels[0], kernels[1], dose)), axis=0))
        inst_grads = jnp.repeat(tile_grads, SLOTS, axis=0)
        unrolled = jax.vmap(lambda plane, offset: jnp.roll(plane, -offset, axis=1))(inst_grads, inst_shift)
        cell_sums = jax.ops.segment_sum(unrolled, cell_ids, num_segments=CELLS)
        squash = jax.nn.sigmoid(cell_params)
        gradient = cell_sums * (2.0 / SLOTS) * squash * (1.0 - squash)
        squares = lax.optimization_barrier(jnp.sum(gradient * gradient, axis=(1, 2)))
        cell_params = cell_params - LR * gradient / jnp.sqrt(squares / (CELL * CELL) + EPS)[:, None, None]
    return cell_params
```

```python
import functools
import math

import jax
import jax.numpy as jnp
import numpy as np
from jax import lax
from jax.experimental import pallas as pl
from jax.experimental.pallas import tpu as pltpu
from jax.sharding import PartitionSpec as P

ITERS = 2
LR = 0.25
EPS = 1e-06
STEEP = 3.0
MESH = pl.DeviceIdType.MESH
HALF = jnp.bfloat16
LINK = jnp.bfloat16


def round_up(value, step):
    return -(-value // step) * step


def layout(count, lanes):
    half = count // 2 + 1
    blocks = max(1, lanes // (2 * half))
    share = -(-count // blocks)
    return half, blocks, share, round_up(share, 16)


def tables(size, count, mid):
    lanes = 2 * mid
    half, blocks, share, tall = layout(count, lanes)
    rows = blocks * tall
    centre = count // 2
    row_of = np.array([f // share * tall + f % share for f in range(count)])

    def placed(matrix):
        result = np.zeros((rows,) + matrix.shape[1:])
        result[row_of] = matrix
        return result

    freqs = np.arange(count) - centre
    phase = (freqs[:, None] * np.arange(size)[None, :] % size) * (2.0 * math.pi / size)
    cos, sin = np.cos(phase), -np.sin(phase)
    fr, fi = placed(cos), placed(sin)
    lr = np.zeros((mid, size))
    li = np.zeros((mid, size))
    lr[:count], li[:count] = cos, sin
    fy = np.zeros((size, lanes))
    fyi = np.zeros((lanes, 2 * size))
    keep = np.zeros((lanes, lanes))
    turned = np.zeros((lanes, lanes))
    for b in range(blocks):
        for g in range(half):
            re = b * 2 * half + g
            im = re + half
            fy[:, re], fy[:, im] = cos[centre + g], sin[centre + g]
            fyi[re] = np.concatenate([cos[centre + g], -sin[centre + g]])
            fyi[im] = np.concatenate([sin[centre + g], cos[centre + g]])
            keep[re, centre + g] = keep[im, mid + centre + g] = 1.0
            if g > 0:
                turned[re, centre - g], turned[im, mid + centre - g] = 1.0, -1.0
    fl = np.concatenate([fr, fi], 0)
    flip = np.zeros((rows, rows))
    flip[row_of, row_of[::-1]] = 1.0
    expand = np.concatenate([keep, turned], 0)
    fold = np.concatenate([keep.T, turned.T], 0)
    flt = fl.T
    gy = np.block([[lr, -li], [li, lr]]) / size
    grid = min(size, round_up(2 * count - 1, 8))
    turn = (freqs[:, None] * np.arange(grid)[None, :] % grid) * (2.0 * math.pi / grid)
    sr, si = placed(np.cos(turn)), placed(-np.sin(turn))
    gl = np.block([[sr.T, si.T], [-si.T, sr.T]]) / size
    gap = np.arange(size)[:, None] / size - np.arange(grid)[None, :] / grid
    band = np.arange(-2 * (count // 2), 2 * (count // 2) + 1)
    wide = np.cos(2.0 * math.pi * band[:, None, None] * gap[None]).sum(0) / grid
    if grid == size:
        wide = np.eye(size)
    parts = dict(fy=fy, fl=fl, fyi=fyi, flt=flt, gy=gy, gyt=gy.T, gl=gl, glt=gl.T, wt=wide.T, flip=flip, expand=expand, fold=fold)
    places, stack, top = {}, [], 0
    for name, t in parts.items():
        places[name] = []
        for left in range(0, t.shape[1], 128):
            piece = t[:, left : left + 128]
            tall = round_up(piece.shape[0], 16)
            places[name].append((top, *piece.shape))
            padded = np.zeros((tall, 128), np.float32)
            padded[: piece.shape[0], : piece.shape[1]] = piece
            stack.append(padded)
            top += tall
    return places, np.concatenate(stack, 0).astype(HALF), wide.astype(np.float32), grid


def dot(a, b):
    return jnp.dot(a.astype(HALF), b.astype(HALF), preferred_element_type=jnp.float32)


def body(sizes, places, theta_hbm, target_hbm, kernels_hbm, dose, owner, local, shift, tabs_hbm, wide_hbm, out,
         theta, target, kernels, tabs, wide, loads, params, wsend, wrecv, kin, krr, kii, near, spectra, psend, precv, gsend, grecv,
         ws, wr, ks, kr, ps, pr, gs, gr):
    n_z, n_x, n_k, count, grid = sizes
    cells, size = theta.shape[0], theta.shape[1]
    slots = local.shape[0] // target.shape[0]
    here = kernels.shape[0] // (2 * count)
    rows, lanes = krr.shape[1], krr.shape[2]
    mid = lanes // 2
    half, blocks, share, tall = layout(count, lanes)
    z, x, k = lax.axis_index("cells"), lax.axis_index("corners"), lax.axis_index("kern")
    zk = [(a, b) for a in range(n_z) for b in range(n_k) if (a, b) != (0, 0)]
    others = [(a, c, b) for a in range(n_z) for c in range(n_x) for b in range(n_k) if (a, c, b) != (0, 0, 0)]

    def at(a, b, c=0):
        return {"cells": lax.rem(z + a, n_z), "corners": lax.rem(x + c, n_x), "kern": lax.rem(k + b, n_k)}

    def send(src, dst, s, r, device):
        copy = pltpu.make_async_remote_copy(
            src_ref=src, dst_ref=dst, send_sem=s, recv_sem=r, device_id=device, device_id_type=MESH
        )
        copy.start()
        return copy

    def table(name):
        pieces = [tabs[top : top + tall, :across] for top, tall, across in places[name]]
        return pieces[0] if len(pieces) == 1 else jnp.concatenate(pieces, 1)

    local_copies = []
    pairs = [(theta_hbm, theta), (tabs_hbm, tabs), (kernels_hbm, kernels), (target_hbm, target), (wide_hbm, wide)]
    for j, (src, dst) in enumerate(pairs):
        copy = pltpu.make_async_copy(src, dst, loads.at[j])
        copy.start()
        local_copies.append(copy)
    barrier = pltpu.get_barrier_semaphore()
    for a, c, b in others:
        pl.semaphore_signal(barrier, inc=1, device_id=at(a, b, c), device_id_type=MESH)

    lane = lax.broadcasted_iota(jnp.int32, (slots, lanes), 1)
    row = lax.broadcasted_iota(jnp.int32, (slots, lanes), 0)
    freq = lane % half
    used = lane < 2 * half * blocks
    offsets = jnp.zeros((slots, lanes), jnp.int32)
    ids = []
    for j in range(slots):
        at_inst = k * slots + j
        offsets = jnp.where(row == j, shift[at_inst], offsets)
        ids.append(owner[at_inst] * cells + local[at_inst])
    turn = lax.rem(freq * offsets, size).astype(jnp.float32) * (2.0 * math.pi / size)
    phr = jnp.where(used, jnp.cos(turn), 0.0) / slots
    phi = jnp.where(used, -jnp.sin(turn), 0.0) / slots
    every = lax.broadcasted_iota(jnp.int32, (n_z * cells, lanes), 0)
    wrr = jnp.zeros((n_z * cells, lanes), jnp.float32)
    wii = jnp.zeros((n_z * cells, lanes), jnp.float32)
    for j in range(slots):
        hit = every == ids[j]
        wrr += jnp.where(hit, phr[j : j + 1], 0.0)
        wii += jnp.where(hit, phi[j : j + 1], 0.0)
    wsend[:, :, :lanes] = wrr.reshape(n_z, cells, lanes)
    wsend[:, :, lanes:] = wii.reshape(n_z, cells, lanes)

    pl.semaphore_wait(barrier, len(others))
    flying = []
    wcopies, kcopies = [], []
    for a, b in zk:
        wcopies.append(send(wsend.at[lax.rem(z + a, n_z)], wrecv.at[a, b], ws.at[a, b], wr.at[a, b], at(a, b)))
    for b in range(1, n_k):
        kcopies.append(send(kernels_hbm, kin.at[b], ks.at[b], kr.at[b], at(0, b)))
    wrecv[0, 0] = wsend[z]
    flying += wcopies + kcopies

    lane = lax.broadcasted_iota(jnp.int32, (rows, lanes), 1)
    sign = jnp.where(lane < mid, -1.0, 1.0)
    lane = lane[:tall]
    block = lane // (2 * half)
    is_real = lane % (2 * half) < half

    def times_i(value):
        return sign * pltpu.roll(value, mid, 1)

    def packed_times_i(value):
        return jnp.where(is_real, -pltpu.roll(value, lanes - half, 1), pltpu.roll(value, half, 1))

    def gather_blocks(value):
        result = value[:tall]
        for b in range(1, blocks):
            result = jnp.where(block == b, value[b * tall : (b + 1) * tall], result)
        return result

    def part_blocks(value):
        return jnp.concatenate([jnp.where(block == b, value, 0.0) for b in range(blocks)], 0)

    first_lane = lax.broadcasted_iota(jnp.int32, (size, lanes), 1)
    centre = jnp.where((first_lane % (2 * half) == 0) & (first_lane < 2 * half * blocks), float(size), 0.0)

    def cell_spectra(source):
        for c in range(cells):
            mask = jax.nn.sigmoid(source[c]).astype(HALF)
            right = 2.0 * dot(mask, table("fy")) - centre
            both = dot(table("fl"), right)
            spectra[c] = gather_blocks(both[:rows]) + packed_times_i(gather_blocks(both[rows:]))

    def spread(source, base):
        for part, wider in ((0, krr), (1, kii)):
            for j in range(here):
                first = (part * here + j) * count
                wider[base + j] = jnp.zeros((rows, lanes), jnp.float32)
                for b in range(blocks):
                    many = min(share, count - b * share)
                    wider[base + j, b * tall : b * tall + many, :count] = (
                        source[first + b * share : first + b * share + many]
                    )
                value = wider[base + j]
                wider[base + j] = value + pltpu.roll(value, mid, 1)

    for copy in local_copies[:2]:
        copy.wait()
    cell_spectra(theta)
    for copy in local_copies[2:]:
        copy.wait()
    spread(kernels, 0)
    for copy in wcopies:
        copy.wait_recv()

    chunk = math.gcd(12, here * n_k)
    steps = here * n_k // chunk
    wanted = target[k].astype(jnp.float32)
    dose_now = dose[0]

    for it in range(ITERS):
        source = theta if it == 0 else params
        if it > 0:
            cell_spectra(source)
        totals = [jnp.zeros((tall, lanes), jnp.float32) for a in range(n_z)]
        for c in range(cells):
            value = spectra[c]
            turned = packed_times_i(value)
            for a in range(n_z):
                w = wrecv[a, 0, c : c + 1]
                totals[a] += w[:, :lanes] * value + w[:, lanes:] * turned
        pcopies = []
        for a in range(1, n_z):
            psend[it, a] = totals[a].astype(LINK)
            pcopies.append(send(psend.at[it, a], precv.at[it, a], ps.at[it, a], pr.at[it, a],
                                {"cells": lax.rem(z - a + n_z, n_z)}))
        flying += pcopies
        spec = totals[0]
        if it == 0:
            for b, copy in zip(range(1, n_k), kcopies):
                copy.wait_recv()
                spread(kin.at[b], b * here)
        for a in range(1, n_z):
            pcopies[a - 1].wait_recv()
            spec += precv[it, a].astype(jnp.float32)
        spec = part_blocks(spec).astype(HALF)
        spec = dot(jnp.concatenate([spec, dot(table("flip"), spec).astype(HALF)], 1), table("expand"))
        turned_spec = times_i(spec)

        def forward(step, image):
            resp = []
            for j in range(chunk):
                at_k = step * chunk + j
                resp.append((krr[at_k] * spec + kii[at_k] * turned_spec).astype(HALF))
            half = dot(jnp.concatenate(resp, 0), table("gy")).astype(HALF)
            for j in range(chunk):
                one = half[j * rows : (j + 1) * rows]
                stacked = jnp.concatenate([one[:, :size], one[:, size:]], 0)
                both = dot(table("gl"), stacked)
                near[step * chunk + j] = both.astype(HALF)
                image += both[:grid] * both[:grid] + both[grid:] * both[grid:]
            return image

        image = lax.fori_loop(0, steps, forward, jnp.zeros((grid, size), jnp.float32))
        image = jnp.dot(wide[...], image, precision=lax.Precision.HIGHEST, preferred_element_type=jnp.float32)
        resist = jax.nn.sigmoid(STEEP * (dose_now * image - 1.0))
        pressure = (4.0 * STEEP) * dose_now * (resist - wanted) * resist * (1.0 - resist)
        pressure = dot(table("wt"), pressure)
        pressure = jnp.concatenate([pressure, pressure], 0)

        def backward(step, sums):
            first, second = sums
            halves = []
            for j in range(chunk):
                both = near[step * chunk + j].astype(jnp.float32) * pressure
                left = dot(table("glt"), both).astype(HALF)
                halves.append(jnp.concatenate([left[:rows], left[rows:]], 1))
            right = dot(jnp.concatenate(halves, 0), table("gyt"))
            for j in range(chunk):
                at_k = step * chunk + j
                one = right[j * rows : (j + 1) * rows]
                first += krr[at_k] * one
                second += kii[at_k] * one
            return first, second

        zero = jnp.zeros((rows, lanes), jnp.float32)
        first, second = lax.fori_loop(0, steps, backward, (zero, zero))
        tile = first - times_i(second)
        tile = tile.astype(HALF)
        tile = dot(jnp.concatenate([tile, dot(table("flip"), tile).astype(HALF)], 1), table("fold"))
        tile = gather_blocks(tile)
        gsend[it] = tile.astype(LINK)
        gcopies = {}
        for a, c, b in others:
            gcopies[a, c, b] = send(gsend.at[it], grecv.at[it, a, c, b], gs.at[it, a, c, b], gr.at[it, a, c, b], at(a, b, c))
        flying += list(gcopies.values())
        sums = [jnp.zeros((tall, lanes), jnp.float32) for c in range(cells)]
        for a, b in [(0, 0)] + zk:
            for c in range(n_x):
                if (a, c, b) != (0, 0, 0):
                    gcopies[a, c, b].wait_recv()
                    part = grecv[it, a, c, b].astype(jnp.float32)
                    tile = part if c == 0 else tile + part
            turned = packed_times_i(tile)
            for c in range(cells):
                w = wrecv[a, b, c : c + 1]
                sums[c] += w[:, :lanes] * tile - w[:, lanes:] * turned
        right = dot(jnp.concatenate([part_blocks(one) for one in sums], 0), table("fyi")).astype(HALF)
        for c in range(cells):
            one = right[c * rows : (c + 1) * rows]
            plane = dot(table("flt"), jnp.concatenate([one[:, :size], one[:, size:]], 0))
            now = source[c]
            squash = jax.nn.sigmoid(now)
            grad = 2.0 * plane * squash * (1.0 - squash)
            square = jnp.sum(jnp.sum(grad * grad, axis=0, keepdims=True), axis=1, keepdims=True)
            params[c] = now - grad * (LR * lax.rsqrt(square / (size * size) + EPS))
    band = out.shape[1]
    start = pl.multiple_of((x * n_k + k) * band, band)
    out[...] = params[:, pl.ds(start, band), :]
    for copy in flying:
        copy.wait_send()


def per_device(theta, target, kernels, dose, inst_owner, inst_local, inst_shift):
    n_z, n_x, n_k = lax.axis_size("cells"), lax.axis_size("corners"), lax.axis_size("kern")
    cells, size = theta.shape[0], theta.shape[1]
    count = kernels.shape[3]
    here = kernels.shape[2]
    assert target.shape[0] == n_k
    mid = round_up(count, 64)
    lanes = 2 * mid
    half, blocks, share, tall = layout(count, lanes)
    rows = blocks * tall
    places, tabs, wide, grid = tables(size, count, mid)
    kernels = kernels.reshape(2 * here * count, count)
    f32, dma = jnp.float32, pltpu.SemaphoreType.DMA
    hbm = pl.BlockSpec(memory_space=pltpu.HBM)
    vmem, smem = pl.BlockSpec(memory_space=pltpu.VMEM), pl.BlockSpec(memory_space=pltpu.SMEM)
    return pl.pallas_call(
        functools.partial(body, (n_z, n_x, n_k, count, grid), places),
        out_shape=jax.ShapeDtypeStruct((cells, size // (n_x * n_k), size), f32),
        in_specs=[hbm] * 3 + [smem] * 4 + [hbm] * 2,
        out_specs=vmem,
        scratch_shapes=[
            pltpu.VMEM(theta.shape, theta.dtype),
            pltpu.VMEM(target.shape, target.dtype),
            pltpu.VMEM(kernels.shape, f32),
            pltpu.VMEM(tabs.shape, tabs.dtype),
            pltpu.VMEM(wide.shape, f32),
            dma((5,)),
            pltpu.VMEM((cells, size, size), f32),
            pltpu.VMEM((n_z, cells, 2 * lanes), f32),
            pltpu.VMEM((n_z, n_k, cells, 2 * lanes), f32),
            pltpu.VMEM((n_k,) + kernels.shape, f32),
            pltpu.VMEM((n_k * here, rows, lanes), f32),
            pltpu.VMEM((n_k * here, rows, lanes), f32),
            pltpu.VMEM((n_k * here, 2 * grid, size), HALF),
            pltpu.VMEM((cells, tall, lanes), f32),
            pltpu.VMEM((ITERS, n_z, tall, lanes), LINK),
            pltpu.VMEM((ITERS, n_z, tall, lanes), LINK),
            pltpu.VMEM((ITERS, tall, lanes), LINK),
            pltpu.VMEM((ITERS, n_z, n_x, n_k, tall, lanes), LINK),
            dma((n_z, n_k)), dma((n_z, n_k)),
            dma((n_k,)), dma((n_k,)),
            dma((ITERS, n_z)), dma((ITERS, n_z)),
            dma((ITERS, n_z, n_x, n_k)), dma((ITERS, n_z, n_x, n_k)),
        ],
        compiler_params=pltpu.CompilerParams(
            collective_id=0, has_side_effects=True, vmem_limit_bytes=63 * 1024 * 1024
        ),
        cost_estimate=pl.CostEstimate(flops=10**9, bytes_accessed=10**7, transcendentals=10**6),
    )(theta, target, kernels, dose, inst_owner.reshape(-1), inst_local, inst_shift, jnp.asarray(tabs), jnp.asarray(wide))


def solution(mesh):
    in_specs = (
        P(("groups", "cells"), None, None),
        P(("groups", "cells"), None, None),
        P(None, "corners", "kern", None, None),
        P("corners"),
        P(("groups", "cells"), None),
        P(("groups", "cells")),
        P(("groups", "cells")),
    )
    out_specs = P(("groups", "cells"), ("corners", "kern"), None)
    return jax.shard_map(
        per_device, mesh=mesh, in_specs=in_specs, out_specs=out_specs, check_vma=False
    )
```

```python
import functools
import math

import jax
import jax.numpy as jnp
import numpy as np
from jax import lax
from jax.experimental import pallas as pl
from jax.experimental.pallas import tpu as pltpu
from jax.sharding import PartitionSpec as P

ITERS = 2
LR = 0.25
EPS = 1e-06
STEEP = 3.0
MESH = pl.DeviceIdType.MESH
HALF = jnp.bfloat16
LINK = jnp.bfloat16


def round_up(value, step):
    return -(-value // step) * step


def layout(count, lanes):
    half = count // 2 + 1
    blocks = max(1, lanes // (2 * half))
    share = -(-count // blocks)
    return half, blocks, share, round_up(share, 16)


def tables(size, count, mid):
    lanes = 2 * mid
    half, blocks, share, tall = layout(count, lanes)
    rows = blocks * tall
    centre = count // 2
    row_of = np.array([f // share * tall + f % share for f in range(count)])

    def placed(matrix):
        result = np.zeros((rows,) + matrix.shape[1:])
        result[row_of] = matrix
        return result

    freqs = np.arange(count) - centre
    phase = (freqs[:, None] * np.arange(size)[None, :] % size) * (2.0 * math.pi / size)
    cos, sin = np.cos(phase), -np.sin(phase)
    fr, fi = placed(cos), placed(sin)
    lr = np.zeros((mid, size))
    li = np.zeros((mid, size))
    lr[:count], li[:count] = cos, sin
    fy = np.zeros((size, lanes))
    fyi = np.zeros((lanes, 2 * size))
    keep = np.zeros((lanes, lanes))
    turned = np.zeros((lanes, lanes))
    for b in range(blocks):
        for g in range(half):
            re = b * 2 * half + g
            im = re + half
            fy[:, re], fy[:, im] = cos[centre + g], sin[centre + g]
            fyi[re] = np.concatenate([cos[centre + g], -sin[centre + g]])
            fyi[im] = np.concatenate([sin[centre + g], cos[centre + g]])
            keep[re, centre + g] = keep[im, mid + centre + g] = 1.0
            if g > 0:
                turned[re, centre - g], turned[im, mid + centre - g] = 1.0, -1.0
    fl = np.concatenate([fr, fi], 0)
    flip = np.zeros((rows, rows))
    flip[row_of, row_of[::-1]] = 1.0
    expand = np.concatenate([keep, turned], 0)
    fold = np.concatenate([keep.T, turned.T], 0)
    flt = fl.T
    gy = np.block([[lr, -li], [li, lr]]) / size
    grid = min(size, round_up(2 * count - 1, 8))
    turn = (freqs[:, None] * np.arange(grid)[None, :] % grid) * (2.0 * math.pi / grid)
    sr, si = placed(np.cos(turn)), placed(-np.sin(turn))
    gl = np.block([[sr.T, si.T], [-si.T, sr.T]]) / size
    gap = np.arange(size)[:, None] / size - np.arange(grid)[None, :] / grid
    band = np.arange(-2 * (count // 2), 2 * (count // 2) + 1)
    wide = np.cos(2.0 * math.pi * band[:, None, None] * gap[None]).sum(0) / grid
    if grid == size:
        wide = np.eye(size)
    parts = dict(fy=fy, fl=fl, fyi=fyi, flt=flt, gy=gy, gyt=gy.T, gl=gl, glt=gl.T, wt=wide.T, flip=flip, expand=expand, fold=fold)
    places, stack, top = {}, [], 0
    for name, t in parts.items():
        places[name] = []
        for left in range(0, t.shape[1], 128):
            piece = t[:, left : left + 128]
            tall = round_up(piece.shape[0], 16)
            places[name].append((top, *piece.shape))
            padded = np.zeros((tall, 128), np.float32)
            padded[: piece.shape[0], : piece.shape[1]] = piece
            stack.append(padded)
            top += tall
    return places, np.concatenate(stack, 0).astype(HALF), wide.astype(np.float32), grid


def dot(a, b):
    return jnp.dot(a.astype(HALF), b.astype(HALF), preferred_element_type=jnp.float32)


def body(sizes, places, theta_hbm, target_hbm, kernels_hbm, dose, owner, local, shift, tabs_hbm, wide_hbm, out,
         theta, target, kernels, tabs, wide, loads, params, slope, wsend, wrecv, kin, krr, kii, near, spectra, psend, precv, gsend, grecv,
         ws, wr, ks, kr, ps, pr, gs, gr):
    n_z, n_x, n_k, count, grid = sizes
    cells, size = theta.shape[0], theta.shape[1]
    slots = local.shape[0] // target.shape[0]
    here = kernels.shape[0] // (2 * count)
    rows, lanes = krr.shape[1], krr.shape[2]
    mid = lanes // 2
    half, blocks, share, tall = layout(count, lanes)
    z, x, k = lax.axis_index("cells"), lax.axis_index("corners"), lax.axis_index("kern")
    zk = [(a, b) for a in range(n_z) for b in range(n_k) if (a, b) != (0, 0)]
    others = [(a, c, b) for a in range(n_z) for c in range(n_x) for b in range(n_k) if (a, c, b) != (0, 0, 0)]

    def at(a, b, c=0):
        return {"cells": lax.rem(z + a, n_z), "corners": lax.rem(x + c, n_x), "kern": lax.rem(k + b, n_k)}

    def send(src, dst, s, r, device):
        copy = pltpu.make_async_remote_copy(
            src_ref=src, dst_ref=dst, send_sem=s, recv_sem=r, device_id=device, device_id_type=MESH
        )
        copy.start()
        return copy

    def table(name):
        pieces = [tabs[top : top + tall, :across] for top, tall, across in places[name]]
        return pieces[0] if len(pieces) == 1 else jnp.concatenate(pieces, 1)

    local_copies = []
    pairs = [(theta_hbm, theta), (tabs_hbm, tabs), (kernels_hbm, kernels), (target_hbm, target), (wide_hbm, wide)]
    for j, (src, dst) in enumerate(pairs):
        copy = pltpu.make_async_copy(src, dst, loads.at[j])
        copy.start()
        local_copies.append(copy)
    barrier = pltpu.get_barrier_semaphore()
    for a, c, b in others:
        pl.semaphore_signal(barrier, inc=1, device_id=at(a, b, c), device_id_type=MESH)

    lane = lax.broadcasted_iota(jnp.int32, (slots, lanes), 1)
    row = lax.broadcasted_iota(jnp.int32, (slots, lanes), 0)
    freq = lane % half
    used = lane < 2 * half * blocks
    offsets = jnp.zeros((slots, lanes), jnp.int32)
    ids = []
    for j in range(slots):
        at_inst = k * slots + j
        offsets = jnp.where(row == j, shift[at_inst], offsets)
        ids.append(owner[at_inst] * cells + local[at_inst])
    turn = lax.rem(freq * offsets, size).astype(jnp.float32) * (2.0 * math.pi / size)
    phr = jnp.where(used, jnp.cos(turn), 0.0) / slots
    phi = jnp.where(used, -jnp.sin(turn), 0.0) / slots
    every = lax.broadcasted_iota(jnp.int32, (n_z * cells, lanes), 0)
    wrr = jnp.zeros((n_z * cells, lanes), jnp.float32)
    wii = jnp.zeros((n_z * cells, lanes), jnp.float32)
    for j in range(slots):
        hit = every == ids[j]
        wrr += jnp.where(hit, phr[j : j + 1], 0.0)
        wii += jnp.where(hit, phi[j : j + 1], 0.0)
    wsend[:, :, :lanes] = wrr.reshape(n_z, cells, lanes)
    wsend[:, :, lanes:] = wii.reshape(n_z, cells, lanes)

    pl.semaphore_wait(barrier, len(others))
    flying = []
    wcopies, kcopies = [], []
    for a, b in zk:
        wcopies.append(send(wsend.at[lax.rem(z + a, n_z)], wrecv.at[a, b], ws.at[a, b], wr.at[a, b], at(a, b)))
    for b in range(1, n_k):
        kcopies.append(send(kernels_hbm, kin.at[b], ks.at[b], kr.at[b], at(0, b)))
    wrecv[0, 0] = wsend[z]
    flying += wcopies + kcopies

    lane = lax.broadcasted_iota(jnp.int32, (rows, lanes), 1)
    sign = jnp.where(lane < mid, -1.0, 1.0)
    lane = lane[:tall]
    block = lane // (2 * half)
    is_real = lane % (2 * half) < half

    def times_i(value):
        return sign * pltpu.roll(value, mid, 1)

    def packed_times_i(value):
        return jnp.where(is_real, -pltpu.roll(value, lanes - half, 1), pltpu.roll(value, half, 1))

    def gather_blocks(value):
        result = value[:tall]
        for b in range(1, blocks):
            result = jnp.where(block == b, value[b * tall : (b + 1) * tall], result)
        return result

    def part_blocks(value):
        return jnp.concatenate([jnp.where(block == b, value, 0.0) for b in range(blocks)], 0)

    first_lane = lax.broadcasted_iota(jnp.int32, (size, lanes), 1)
    pair = math.gcd(2, cells)
    centre = jnp.where((first_lane % (2 * half) == 0) & (first_lane < 2 * half * blocks), float(size), 0.0)

    def cell_spectra(source):
        right = []
        for c in range(cells):
            squash = jax.nn.sigmoid(source[c])
            right.append((2.0 * dot(squash, table("fy")) - centre).astype(HALF))
        for c in range(0, cells, pair):
            wider = dot(table("fl"), jnp.concatenate(right[c : c + pair], 1))
            for j in range(pair):
                both = wider[:, j * lanes : (j + 1) * lanes]
                spectra[c + j] = gather_blocks(both[:rows]) + packed_times_i(gather_blocks(both[rows:]))

    def spread(source, base):
        for part, wider in ((0, krr), (1, kii)):
            for j in range(here):
                first = (part * here + j) * count
                wider[base + j] = jnp.zeros((rows, lanes), jnp.float32)
                for b in range(blocks):
                    many = min(share, count - b * share)
                    wider[base + j, b * tall : b * tall + many, :count] = (
                        source[first + b * share : first + b * share + many]
                    )
                value = wider[base + j]
                wider[base + j] = value + pltpu.roll(value, mid, 1)

    for copy in local_copies[:2]:
        copy.wait()
    cell_spectra(theta)
    for copy in local_copies[2:]:
        copy.wait()
    spread(kernels, 0)
    for copy in wcopies:
        copy.wait_recv()

    chunk = math.gcd(12, here * n_k)
    pair_k = math.gcd(2, chunk)
    steps = here * n_k // chunk
    wanted = target[k].astype(jnp.float32)
    dose_now = dose[0]

    for it in range(ITERS):
        source = theta if it == 0 else params
        if it > 0:
            cell_spectra(source)
        totals = [jnp.zeros((tall, lanes), jnp.float32) for a in range(n_z)]
        for c in range(cells):
            value = spectra[c]
            turned = packed_times_i(value)
            for a in range(n_z):
                w = wrecv[a, 0, c : c + 1]
                totals[a] += w[:, :lanes] * value + w[:, lanes:] * turned
        pcopies = []
        for a in range(1, n_z):
            psend[it, a] = totals[a].astype(LINK)
            pcopies.append(send(psend.at[it, a], precv.at[it, a], ps.at[it, a], pr.at[it, a],
                                {"cells": lax.rem(z - a + n_z, n_z)}))
        flying += pcopies
        spec = totals[0]
        if it == 0:
            for b, copy in zip(range(1, n_k), kcopies):
                copy.wait_recv()
                spread(kin.at[b], b * here)
        for a in range(1, n_z):
            pcopies[a - 1].wait_recv()
            spec += precv[it, a].astype(jnp.float32)
        spec = part_blocks(spec).astype(HALF)
        spec = dot(jnp.concatenate([spec, dot(table("flip"), spec).astype(HALF)], 1), table("expand"))
        turned_spec = times_i(spec)

        def forward(step, image):
            resp = []
            for j in range(chunk):
                at_k = step * chunk + j
                resp.append((krr[at_k] * spec + kii[at_k] * turned_spec).astype(HALF))
            wave = dot(jnp.concatenate(resp, 0), table("gy")).astype(HALF)
            for j in range(0, chunk, pair_k):
                ones = [wave[i * rows : (i + 1) * rows] for i in range(j, j + pair_k)]
                stacked = jnp.concatenate(
                    [
                        jnp.concatenate([one[:, :size] for one in ones], 1),
                        jnp.concatenate([one[:, size:] for one in ones], 1),
                    ],
                    0,
                )
                both = dot(table("gl"), stacked)
                near[(step * chunk + j) // pair_k] = both.astype(HALF)
                image += both[:grid] * both[:grid] + both[grid:] * both[grid:]
            return image

        image = lax.fori_loop(0, steps, forward, jnp.zeros((grid, pair_k * size), jnp.float32))
        image = sum(image[:, j * size : (j + 1) * size] for j in range(pair_k))
        image = jnp.dot(wide[...], image, precision=lax.Precision.HIGHEST, preferred_element_type=jnp.float32)
        resist = jax.nn.sigmoid(STEEP * (dose_now * image - 1.0))
        pressure = (4.0 * STEEP) * dose_now * (resist - wanted) * resist * (1.0 - resist)
        pressure = dot(table("wt"), pressure)
        pressure = jnp.concatenate([jnp.concatenate([pressure] * pair_k, 1)] * 2, 0)

        def backward(step, sums):
            first, second = sums
            halves = []
            for j in range(0, chunk, pair_k):
                both = near[(step * chunk + j) // pair_k].astype(jnp.float32) * pressure
                left = dot(table("glt"), both).astype(HALF)
                for i in range(pair_k):
                    one = left[:, i * size : (i + 1) * size]
                    halves.append(jnp.concatenate([one[:rows], one[rows:]], 1))
            right = dot(jnp.concatenate(halves, 0), table("gyt"))
            for j in range(chunk):
                at_k = step * chunk + j
                one = right[j * rows : (j + 1) * rows]
                first += krr[at_k] * one
                second += kii[at_k] * one
            return first, second

        zero = jnp.zeros((rows, lanes), jnp.float32)
        first, second = lax.fori_loop(0, steps, backward, (zero, zero))
        tile = first - times_i(second)
        tile = tile.astype(HALF)
        tile = dot(jnp.concatenate([tile, dot(table("flip"), tile).astype(HALF)], 1), table("fold"))
        tile = gather_blocks(tile)
        gsend[it] = tile.astype(LINK)
        gcopies = {}
        for a, c, b in others:
            gcopies[a, c, b] = send(gsend.at[it], grecv.at[it, a, c, b], gs.at[it, a, c, b], gr.at[it, a, c, b], at(a, b, c))
        flying += list(gcopies.values())
        for c in range(cells):
            squash = jax.nn.sigmoid(source[c])
            slope[c] = 2.0 * squash * (1.0 - squash)
        sums = [jnp.zeros((tall, lanes), jnp.float32) for c in range(cells)]
        for a, b in [(0, 0)] + zk:
            for c in range(n_x):
                if (a, c, b) != (0, 0, 0):
                    gcopies[a, c, b].wait_recv()
                    part = grecv[it, a, c, b].astype(jnp.float32)
                    tile = part if c == 0 else tile + part
            turned = packed_times_i(tile)
            for c in range(cells):
                w = wrecv[a, b, c : c + 1]
                sums[c] += w[:, :lanes] * tile - w[:, lanes:] * turned
        right = dot(jnp.concatenate([part_blocks(one) for one in sums], 0), table("fyi")).astype(HALF)
        for c in range(0, cells, pair):
            ones = [right[i * rows : (i + 1) * rows] for i in range(c, c + pair)]
            stacked = jnp.concatenate(
                [
                    jnp.concatenate([one[:, :size] for one in ones], 1),
                    jnp.concatenate([one[:, size:] for one in ones], 1),
                ],
                0,
            )
            planes = dot(table("flt"), stacked)
            for j in range(pair):
                grad = planes[:, j * size : (j + 1) * size] * slope[c + j]
                square = jnp.sum(jnp.sum(grad * grad, axis=0, keepdims=True), axis=1, keepdims=True)
                params[c + j] = source[c + j] - grad * (LR * lax.rsqrt(square / (size * size) + EPS))
    band = out.shape[1]
    start = pl.multiple_of((x * n_k + k) * band, band)
    out[...] = params[:, pl.ds(start, band), :]
    for copy in flying:
        copy.wait_send()


def per_device(theta, target, kernels, dose, inst_owner, inst_local, inst_shift):
    n_z, n_x, n_k = lax.axis_size("cells"), lax.axis_size("corners"), lax.axis_size("kern")
    cells, size = theta.shape[0], theta.shape[1]
    count = kernels.shape[3]
    here = kernels.shape[2]
    assert target.shape[0] == n_k
    mid = round_up(count, 64)
    lanes = 2 * mid
    half, blocks, share, tall = layout(count, lanes)
    rows = blocks * tall
    places, tabs, wide, grid = tables(size, count, mid)
    kernels = kernels.reshape(2 * here * count, count)
    pair_k = math.gcd(2, n_k * here)
    f32, dma = jnp.float32, pltpu.SemaphoreType.DMA
    hbm = pl.BlockSpec(memory_space=pltpu.HBM)
    vmem, smem = pl.BlockSpec(memory_space=pltpu.VMEM), pl.BlockSpec(memory_space=pltpu.SMEM)
    return pl.pallas_call(
        functools.partial(body, (n_z, n_x, n_k, count, grid), places),
        out_shape=jax.ShapeDtypeStruct((cells, size // (n_x * n_k), size), f32),
        in_specs=[hbm] * 3 + [smem] * 4 + [hbm] * 2,
        out_specs=vmem,
        scratch_shapes=[
            pltpu.VMEM(theta.shape, theta.dtype),
            pltpu.VMEM(target.shape, target.dtype),
            pltpu.VMEM(kernels.shape, f32),
            pltpu.VMEM(tabs.shape, tabs.dtype),
            pltpu.VMEM(wide.shape, f32),
            dma((5,)),
            pltpu.VMEM((cells, size, size), f32),
            pltpu.VMEM((cells, size, size), f32),
            pltpu.VMEM((n_z, cells, 2 * lanes), f32),
            pltpu.VMEM((n_z, n_k, cells, 2 * lanes), f32),
            pltpu.VMEM((n_k,) + kernels.shape, f32),
            pltpu.VMEM((n_k * here, rows, lanes), f32),
            pltpu.VMEM((n_k * here, rows, lanes), f32),
            pltpu.VMEM((n_k * here // pair_k, 2 * grid, pair_k * size), HALF),
            pltpu.VMEM((cells, tall, lanes), f32),
            pltpu.VMEM((ITERS, n_z, tall, lanes), LINK),
            pltpu.VMEM((ITERS, n_z, tall, lanes), LINK),
            pltpu.VMEM((ITERS, tall, lanes), LINK),
            pltpu.VMEM((ITERS, n_z, n_x, n_k, tall, lanes), LINK),
            dma((n_z, n_k)), dma((n_z, n_k)),
            dma((n_k,)), dma((n_k,)),
            dma((ITERS, n_z)), dma((ITERS, n_z)),
            dma((ITERS, n_z, n_x, n_k)), dma((ITERS, n_z, n_x, n_k)),
        ],
        compiler_params=pltpu.CompilerParams(
            collective_id=0, has_side_effects=True, vmem_limit_bytes=63 * 1024 * 1024
        ),
        cost_estimate=pl.CostEstimate(flops=10**9, bytes_accessed=10**7, transcendentals=10**6),
    )(theta, target, kernels, dose, inst_owner.reshape(-1), inst_local, inst_shift, jnp.asarray(tabs), jnp.asarray(wide))


def solution(mesh):
    in_specs = (
        P(("groups", "cells"), None, None),
        P(("groups", "cells"), None, None),
        P(None, "corners", "kern", None, None),
        P("corners"),
        P(("groups", "cells"), None),
        P(("groups", "cells")),
        P(("groups", "cells")),
    )
    out_specs = P(("groups", "cells"), ("corners", "kern"), None)
    return jax.shard_map(
        per_device, mesh=mesh, in_specs=in_specs, out_specs=out_specs, check_vma=False
    )
```

```python
import functools
import math

import jax
import jax.numpy as jnp
import numpy as np
from jax import lax
from jax.experimental import pallas as pl
from jax.experimental.pallas import tpu as pltpu
from jax.sharding import PartitionSpec as P

ITERS = 2
LR = 0.25
EPS = 1e-06
STEEP = 3.0
MESH = pl.DeviceIdType.MESH
HALF = jnp.bfloat16
LINK = jnp.bfloat16


def round_up(value, step):
    return -(-value // step) * step


def layout(count, lanes):
    half = count // 2 + 1
    blocks = max(1, lanes // (2 * half))
    share = -(-count // blocks)
    return half, blocks, share, round_up(share, 16)


def tables(size, count, mid):
    lanes = 2 * mid
    half, blocks, share, tall = layout(count, lanes)
    rows = blocks * tall
    centre = count // 2
    row_of = np.array([f // share * tall + f % share for f in range(count)])

    def placed(matrix):
        result = np.zeros((rows,) + matrix.shape[1:])
        result[row_of] = matrix
        return result

    freqs = np.arange(count) - centre
    phase = (freqs[:, None] * np.arange(size)[None, :] % size) * (2.0 * math.pi / size)
    cos, sin = np.cos(phase), -np.sin(phase)
    fr, fi = placed(cos), placed(sin)
    lr = np.zeros((mid, size))
    li = np.zeros((mid, size))
    lr[:count], li[:count] = cos, sin
    fy = np.zeros((size, lanes))
    fyi = np.zeros((lanes, 2 * size))
    keep = np.zeros((lanes, lanes))
    turned = np.zeros((lanes, lanes))
    for b in range(blocks):
        for g in range(half):
            re = b * 2 * half + g
            im = re + half
            fy[:, re], fy[:, im] = cos[centre + g], sin[centre + g]
            fyi[re] = np.concatenate([cos[centre + g], -sin[centre + g]])
            fyi[im] = np.concatenate([sin[centre + g], cos[centre + g]])
            keep[re, centre + g] = keep[im, mid + centre + g] = 1.0
            if g > 0:
                turned[re, centre - g], turned[im, mid + centre - g] = 1.0, -1.0
    fl = np.concatenate([fr, fi], 0)
    flip = np.zeros((rows, rows))
    flip[row_of, row_of[::-1]] = 1.0
    expand = np.concatenate([keep, turned], 0)
    fold = np.concatenate([keep.T, turned.T], 0)
    flt = fl.T
    gy = np.block([[lr, -li], [li, lr]]) / size
    grid = min(size, round_up(2 * count - 1, 8))
    turn = (freqs[:, None] * np.arange(grid)[None, :] % grid) * (2.0 * math.pi / grid)
    sr, si = placed(np.cos(turn)), placed(-np.sin(turn))
    gl = np.block([[sr.T, si.T], [-si.T, sr.T]]) / size
    gap = np.arange(size)[:, None] / size - np.arange(grid)[None, :] / grid
    band = np.arange(-2 * (count // 2), 2 * (count // 2) + 1)
    wide = np.cos(2.0 * math.pi * band[:, None, None] * gap[None]).sum(0) / grid
    if grid == size:
        wide = np.eye(size)
    wide_hi = wide.astype(HALF).astype(np.float64)
    parts = dict(fy=fy, fl=fl, fyi=fyi, flt=flt, gy=gy, gyt=gy.T, gl=gl, glt=gl.T, wide=np.concatenate([wide_hi, wide - wide_hi, wide_hi], 1), wt=wide.T, flip=flip, expand=expand, fold=fold)
    places, stack, top = {}, [], 0
    for name, t in parts.items():
        places[name] = []
        for left in range(0, t.shape[1], 128):
            piece = t[:, left : left + 128]
            tall = round_up(piece.shape[0], 16)
            places[name].append((top, *piece.shape))
            padded = np.zeros((tall, 128), np.float32)
            padded[: piece.shape[0], : piece.shape[1]] = piece
            stack.append(padded)
            top += tall
    return places, np.concatenate(stack, 0).astype(HALF), grid


def dot(a, b):
    return jnp.dot(a.astype(HALF), b.astype(HALF), preferred_element_type=jnp.float32)


def body(sizes, places, theta_hbm, target_hbm, kernels_hbm, dose, owner, local, shift, tabs_hbm, out,
         theta, target, kernels, tabs, loads, params, slope, wsend, wrecv, kin, krr, kii, near, spectra, psend, precv, gsend, grecv,
         ws, wr, ks, kr, ps, pr, gs, gr):
    n_z, n_x, n_k, count, grid = sizes
    cells, size = theta.shape[0], theta.shape[1]
    slots = local.shape[0] // target.shape[0]
    here = kernels.shape[0] // (2 * count)
    rows, lanes = krr.shape[1], krr.shape[2]
    mid = lanes // 2
    half, blocks, share, tall = layout(count, lanes)
    z, x, k = lax.axis_index("cells"), lax.axis_index("corners"), lax.axis_index("kern")
    zk = [(a, b) for a in range(n_z) for b in range(n_k) if (a, b) != (0, 0)]
    others = [(a, c, b) for a in range(n_z) for c in range(n_x) for b in range(n_k) if (a, c, b) != (0, 0, 0)]

    def at(a, b, c=0):
        return {"cells": lax.rem(z + a, n_z), "corners": lax.rem(x + c, n_x), "kern": lax.rem(k + b, n_k)}

    def send(src, dst, s, r, device):
        copy = pltpu.make_async_remote_copy(
            src_ref=src, dst_ref=dst, send_sem=s, recv_sem=r, device_id=device, device_id_type=MESH
        )
        copy.start()
        return copy

    def table(name):
        pieces = [tabs[top : top + tall, :across] for top, tall, across in places[name]]
        return pieces[0] if len(pieces) == 1 else jnp.concatenate(pieces, 1)

    local_copies = []
    pairs = [(theta_hbm, theta), (tabs_hbm, tabs), (kernels_hbm, kernels), (target_hbm, target)]
    for j, (src, dst) in enumerate(pairs):
        copy = pltpu.make_async_copy(src, dst, loads.at[j])
        copy.start()
        local_copies.append(copy)
    barrier = pltpu.get_barrier_semaphore()
    for a, c, b in others:
        pl.semaphore_signal(barrier, inc=1, device_id=at(a, b, c), device_id_type=MESH)

    lane = lax.broadcasted_iota(jnp.int32, (slots, lanes), 1)
    row = lax.broadcasted_iota(jnp.int32, (slots, lanes), 0)
    freq = lane % half
    used = lane < 2 * half * blocks
    offsets = jnp.zeros((slots, lanes), jnp.int32)
    ids = []
    for j in range(slots):
        at_inst = k * slots + j
        offsets = jnp.where(row == j, shift[at_inst], offsets)
        ids.append(owner[at_inst] * cells + local[at_inst])
    turn = lax.rem(freq * offsets, size).astype(jnp.float32) * (2.0 * math.pi / size)
    phr = jnp.where(used, jnp.cos(turn), 0.0) / slots
    phi = jnp.where(used, -jnp.sin(turn), 0.0) / slots
    every = lax.broadcasted_iota(jnp.int32, (n_z * cells, lanes), 0)
    wrr = jnp.zeros((n_z * cells, lanes), jnp.float32)
    wii = jnp.zeros((n_z * cells, lanes), jnp.float32)
    for j in range(slots):
        hit = every == ids[j]
        wrr += jnp.where(hit, phr[j : j + 1], 0.0)
        wii += jnp.where(hit, phi[j : j + 1], 0.0)
    wsend[:, :, :lanes] = wrr.reshape(n_z, cells, lanes)
    wsend[:, :, lanes:] = wii.reshape(n_z, cells, lanes)

    pl.semaphore_wait(barrier, len(others))
    flying = []
    wcopies, kcopies = {}, []
    for a, b in sorted(zk, key=lambda ab: ab[1]):
        wcopies[a, b] = (send(wsend.at[lax.rem(z + a, n_z)], wrecv.at[a, b], ws.at[a, b], wr.at[a, b], at(a, b)))
    for b in range(1, n_k):
        kcopies.append(send(kernels_hbm, kin.at[b], ks.at[b], kr.at[b], at(0, b)))
    wrecv[0, 0] = wsend[z]
    flying += list(wcopies.values()) + kcopies

    lane = lax.broadcasted_iota(jnp.int32, (rows, lanes), 1)
    sign = jnp.where(lane < mid, -1.0, 1.0)
    lane = lane[:tall]
    block = lane // (2 * half)
    is_real = lane % (2 * half) < half

    def times_i(value):
        return sign * pltpu.roll(value, mid, 1)

    def packed_times_i(value):
        return jnp.where(is_real, -pltpu.roll(value, lanes - half, 1), pltpu.roll(value, half, 1))

    def gather_blocks(value):
        result = value[:tall]
        for b in range(1, blocks):
            result = jnp.where(block == b, value[b * tall : (b + 1) * tall], result)
        return result

    def part_blocks(value):
        return jnp.concatenate([jnp.where(block == b, value, 0.0) for b in range(blocks)], 0)

    first_lane = lax.broadcasted_iota(jnp.int32, (size, lanes), 1)
    pair = math.gcd(2, cells)
    centre = jnp.where((first_lane % (2 * half) == 0) & (first_lane < 2 * half * blocks), float(size), 0.0)

    def cell_spectra(source):
        right = []
        for c in range(cells):
            squash = jax.nn.sigmoid(source[c])
            right.append((2.0 * dot(squash, table("fy")) - centre).astype(HALF))
        for c in range(0, cells, pair):
            wider = dot(table("fl"), jnp.concatenate(right[c : c + pair], 1))
            for j in range(pair):
                both = wider[:, j * lanes : (j + 1) * lanes]
                spectra[c + j] = gather_blocks(both[:rows]) + packed_times_i(gather_blocks(both[rows:]))

    def spread(source, base):
        for part, wider in ((0, krr), (1, kii)):
            for j in range(here):
                first = (part * here + j) * count
                wider[base + j] = jnp.zeros((rows, lanes), jnp.float32)
                for b in range(blocks):
                    many = min(share, count - b * share)
                    wider[base + j, b * tall : b * tall + many, :count] = (
                        source[first + b * share : first + b * share + many]
                    )
                value = wider[base + j]
                wider[base + j] = value + pltpu.roll(value, mid, 1)

    for copy in local_copies[:2]:
        copy.wait()
    cell_spectra(theta)
    for copy in local_copies[2:]:
        copy.wait()
    spread(kernels, 0)
    for a in range(1, n_z):
        wcopies[a, 0].wait_recv()

    chunk = math.gcd(6, here * n_k)
    pair_k = math.gcd(2, chunk)
    steps = here * n_k // chunk
    wanted = target[k].astype(jnp.float32)
    dose_now = dose[0]

    for it in range(ITERS):
        source = theta if it == 0 else params
        if it > 0:
            cell_spectra(source)
        values = [spectra[c] for c in range(cells)]
        turned = [packed_times_i(value) for value in values]
        pcopies = {}
        spec = None
        for a in list(range(n_z - 1, -1, -1)):
            total = jnp.zeros((tall, lanes), jnp.float32)
            for c in range(cells):
                w = wrecv[a, 0, c : c + 1]
                total += w[:, :lanes] * values[c] + w[:, lanes:] * turned[c]
            if a == 0:
                spec = total
            else:
                psend[it, a] = total.astype(LINK)
                pcopies[a] = send(psend.at[it, a], precv.at[it, a], ps.at[it, a], pr.at[it, a],
                                  {"cells": lax.rem(z - a + n_z, n_z)})
        flying += list(pcopies.values())
        if it == 0:
            for b, copy in zip(range(1, n_k), kcopies):
                copy.wait_recv()
                spread(kin.at[b], b * here)
        for a in range(1, n_z):
            pcopies[a].wait_recv()
            spec += precv[it, a].astype(jnp.float32)
        spec = part_blocks(spec).astype(HALF)
        spec = dot(jnp.concatenate([spec, dot(table("flip"), spec).astype(HALF)], 1), table("expand"))
        turned_spec = times_i(spec)

        def forward(step, image):
            resp = []
            for j in range(chunk):
                at_k = step * chunk + j
                resp.append((krr[at_k] * spec + kii[at_k] * turned_spec).astype(HALF))
            wave = dot(jnp.concatenate(resp, 0), table("gy")).astype(HALF)
            for j in range(0, chunk, pair_k):
                ones = [wave[i * rows : (i + 1) * rows] for i in range(j, j + pair_k)]
                stacked = jnp.concatenate(
                    [
                        jnp.concatenate([one[:, :size] for one in ones], 1),
                        jnp.concatenate([one[:, size:] for one in ones], 1),
                    ],
                    0,
                )
                both = dot(table("gl"), stacked)
                near[(step * chunk + j) // pair_k] = both.astype(HALF)
                image += both[:grid] * both[:grid] + both[grid:] * both[grid:]
            return image

        image = jnp.zeros((grid, pair_k * size), jnp.float32)
        for step in range(steps):
            image = forward(step, image)
        image = sum(image[:, j * size : (j + 1) * size] for j in range(pair_k))
        coarse = image.astype(HALF).astype(jnp.float32)
        image = dot(table("wide"), jnp.concatenate([coarse, coarse, image - coarse], 0))
        resist = jax.nn.sigmoid(STEEP * (dose_now * image - 1.0))
        pressure = (4.0 * STEEP) * dose_now * (resist - wanted) * resist * (1.0 - resist)
        pressure = dot(table("wt"), pressure)
        pressure = jnp.concatenate([jnp.concatenate([pressure] * pair_k, 1)] * 2, 0)

        def backward(step, sums):
            first, second = sums
            halves = []
            for j in range(0, chunk, pair_k):
                both = near[(step * chunk + j) // pair_k].astype(jnp.float32) * pressure
                left = dot(table("glt"), both).astype(HALF)
                for i in range(pair_k):
                    one = left[:, i * size : (i + 1) * size]
                    halves.append(jnp.concatenate([one[:rows], one[rows:]], 1))
            right = dot(jnp.concatenate(halves, 0), table("gyt"))
            for j in range(chunk):
                at_k = step * chunk + j
                one = right[j * rows : (j + 1) * rows]
                first += krr[at_k] * one
                second += kii[at_k] * one
            return first, second

        zero = jnp.zeros((rows, lanes), jnp.float32)
        first, second = zero, zero
        for step in range(steps):
            first, second = backward(step, (first, second))
        tile = first - times_i(second)
        tile = tile.astype(HALF)
        tile = dot(jnp.concatenate([tile, dot(table("flip"), tile).astype(HALF)], 1), table("fold"))
        tile = gather_blocks(tile)
        gsend[it] = tile.astype(LINK)
        gcopies = {}
        for a, c, b in sorted(others, key=lambda o: (o[0] == 0, -o[0])):
            gcopies[a, c, b] = send(gsend.at[it], grecv.at[it, a, c, b], gs.at[it, a, c, b], gr.at[it, a, c, b], at(a, b, c))
        flying += list(gcopies.values())
        for c in range(cells):
            squash = jax.nn.sigmoid(source[c])
            slope[c] = 2.0 * squash * (1.0 - squash)
        if it == 0:
            for a, b in zk:
                if b > 0:
                    wcopies[a, b].wait_recv()
        sums = [jnp.zeros((tall, lanes), jnp.float32) for c in range(cells)]
        for a, b in [(0, 0)] + zk:
            for c in range(n_x):
                if (a, c, b) != (0, 0, 0):
                    gcopies[a, c, b].wait_recv()
                    part = grecv[it, a, c, b].astype(jnp.float32)
                    tile = part if c == 0 else tile + part
            turned = packed_times_i(tile)
            for c in range(cells):
                w = wrecv[a, b, c : c + 1]
                sums[c] += w[:, :lanes] * tile - w[:, lanes:] * turned
        right = dot(jnp.concatenate([part_blocks(one) for one in sums], 0), table("fyi")).astype(HALF)
        for c in range(0, cells, pair):
            ones = [right[i * rows : (i + 1) * rows] for i in range(c, c + pair)]
            stacked = jnp.concatenate(
                [
                    jnp.concatenate([one[:, :size] for one in ones], 1),
                    jnp.concatenate([one[:, size:] for one in ones], 1),
                ],
                0,
            )
            planes = dot(table("flt"), stacked)
            for j in range(pair):
                grad = planes[:, j * size : (j + 1) * size] * slope[c + j]
                square = jnp.sum(jnp.sum(grad * grad, axis=0, keepdims=True), axis=1, keepdims=True)
                params[c + j] = source[c + j] - grad * (LR * lax.rsqrt(square / (size * size) + EPS))
    band = out.shape[1]
    start = pl.multiple_of((x * n_k + k) * band, band)
    out[...] = params[:, pl.ds(start, band), :]
    for copy in flying:
        copy.wait_send()


def per_device(theta, target, kernels, dose, inst_owner, inst_local, inst_shift):
    n_z, n_x, n_k = lax.axis_size("cells"), lax.axis_size("corners"), lax.axis_size("kern")
    cells, size = theta.shape[0], theta.shape[1]
    count = kernels.shape[3]
    here = kernels.shape[2]
    assert target.shape[0] == n_k
    mid = round_up(count, 64)
    lanes = 2 * mid
    half, blocks, share, tall = layout(count, lanes)
    rows = blocks * tall
    places, tabs, grid = tables(size, count, mid)
    kernels = kernels.reshape(2 * here * count, count)
    pair_k = math.gcd(2, n_k * here)
    f32, dma = jnp.float32, pltpu.SemaphoreType.DMA
    hbm = pl.BlockSpec(memory_space=pltpu.HBM)
    vmem, smem = pl.BlockSpec(memory_space=pltpu.VMEM), pl.BlockSpec(memory_space=pltpu.SMEM)
    return pl.pallas_call(
        functools.partial(body, (n_z, n_x, n_k, count, grid), places),
        out_shape=jax.ShapeDtypeStruct((cells, size // (n_x * n_k), size), f32),
        in_specs=[hbm] * 3 + [smem] * 4 + [hbm],
        out_specs=vmem,
        scratch_shapes=[
            pltpu.VMEM(theta.shape, theta.dtype),
            pltpu.VMEM(target.shape, target.dtype),
            pltpu.VMEM(kernels.shape, f32),
            pltpu.VMEM(tabs.shape, tabs.dtype),
            dma((4,)),
            pltpu.VMEM((cells, size, size), f32),
            pltpu.VMEM((cells, size, size), f32),
            pltpu.VMEM((n_z, cells, 2 * lanes), f32),
            pltpu.VMEM((n_z, n_k, cells, 2 * lanes), f32),
            pltpu.VMEM((n_k,) + kernels.shape, f32),
            pltpu.VMEM((n_k * here, rows, lanes), f32),
            pltpu.VMEM((n_k * here, rows, lanes), f32),
            pltpu.VMEM((n_k * here // pair_k, 2 * grid, pair_k * size), HALF),
            pltpu.VMEM((cells, tall, lanes), f32),
            pltpu.VMEM((ITERS, n_z, tall, lanes), LINK),
            pltpu.VMEM((ITERS, n_z, tall, lanes), LINK),
            pltpu.VMEM((ITERS, tall, lanes), LINK),
            pltpu.VMEM((ITERS, n_z, n_x, n_k, tall, lanes), LINK),
            dma((n_z, n_k)), dma((n_z, n_k)),
            dma((n_k,)), dma((n_k,)),
            dma((ITERS, n_z)), dma((ITERS, n_z)),
            dma((ITERS, n_z, n_x, n_k)), dma((ITERS, n_z, n_x, n_k)),
        ],
        compiler_params=pltpu.CompilerParams(
            collective_id=0, has_side_effects=True, vmem_limit_bytes=63 * 1024 * 1024
        ),
        cost_estimate=pl.CostEstimate(flops=10**9, bytes_accessed=10**7, transcendentals=10**6),
    )(theta, target, kernels, dose, inst_owner.reshape(-1), inst_local, inst_shift, jnp.asarray(tabs))


def solution(mesh):
    in_specs = (
        P(("groups", "cells"), None, None),
        P(("groups", "cells"), None, None),
        P(None, "corners", "kern", None, None),
        P("corners"),
        P(("groups", "cells"), None),
        P(("groups", "cells")),
        P(("groups", "cells")),
    )
    out_specs = P(("groups", "cells"), ("corners", "kern"), None)
    return jax.shard_map(
        per_device, mesh=mesh, in_specs=in_specs, out_specs=out_specs, check_vma=False
    )
```
